128 devices in a mesh: pool: 16 (over x, y), tp: 8 (over z, core).
Axes of the slice: x: 4, y: 4, z: 4, core: 2. Of those that a mesh axis runs over, the one named last changes fastest.
Arguments:
- tokens: bfloat16 [3072, 8192], P('pool', 'tp'), may hold values from -6 to 6
- w_query: bfloat16 [8192, 8192], P(None, 'tp'), may hold values from -0.0625 to 0.0625
- w_key: bfloat16 [8192, 1024], P(None, 'tp'), may hold values from -0.0625 to 0.0625
- w_value: bfloat16 [8192, 1024], P(None, 'tp'), may hold values from -0.0625 to 0.0625
- kv_pool: bfloat16 [1024, 8, 2, 64, 128], P('pool', 'tp'), may hold values from -42 to 42
- page_owner: int32 [48, 128, 1], P('pool'), may hold values from 0 to 15; in each aligned block of 384 rows (0 to 383, 384 to 767, ..., all dimensions but the last counted through in order) at most 32 rows name the same one
- page_slot: int32 [48, 128], P('pool'), may hold values from 0 to 63
- prefix_len: int32 [48], P('pool'), may hold values from 2048 to 8192, as said below
Outputs:
- attended: bfloat16 [3072, 8192], P('pool', 'tp')
- suffix_kv: bfloat16 [3072, 2, 8, 128], P('pool', None, 'tp')
The draws below stay inside these ranges and needn't reach their ends.
Inputs may be any that keep to these rules, and one draw needn't show every extreme that they name: `page_owner`: within the rows of one index of pool (3 x 128 entries) no owner appears more than 32 times, and some owner appears exactly 32 times. `prefix_len`: some node has exactly 8192 prefix tokens and another exactly 2048.
All inputs are finite; a program needn't handle non-finite values.
Results may differ from the reference program's by a relative error of at most 0.0065.
The reference program's roundings to bfloat16 on the way count: a program that leaves them out, or rounds other values in their place, can miss the bound.
Values may be sent and summed in bfloat16 or wider, within the bound.
No kernel may reach another device: no remote copies, remote signals or barrier semaphores. Data moves between devices by JAX's collectives and lax.ppermute only.
A program may use at most 192 MiB of HBM per device.

```python
import math
import jax
import jax.numpy as jnp
import numpy as np
from jax import lax

D = 8192
QH = 64
KVH = 8
HD = 128
PAGE = 64
SUF = 64
MINP = 32
MAXP = 128
NODES_DEV = 3
SLOTS = 64
NODES = 48
TOKENS = 3072
POOL_PAGES = 1024
CAP = 32
N_POOL = 16


def draw_kv_pool(key, part):
    key = jax.random.fold_in(key, 11)
    second_key = jax.random.fold_in(key, 1)
    shape = (POOL_PAGES, KVH, 2, PAGE, HD)
    values = jnp.clip(jax.random.normal(second_key, shape, jnp.float32), -4.0, 4.0)
    return values.astype(jnp.bfloat16)


def draw_prefix_len(key, part):
    key = jax.random.fold_in(key, 5)
    first_key, second_key, third_key = jax.random.split(key, 3)
    lengths = jax.random.randint(first_key, (NODES,), MINP * PAGE, MAXP * PAGE + 1, dtype=jnp.int32)
    lowest = jax.random.randint(second_key, (), 0, NODES, dtype=jnp.int32)
    highest = (lowest + 1 + jax.random.randint(third_key, (), 0, NODES - 1, dtype=jnp.int32)) % NODES
    lengths = lengths.at[lowest].set(MINP * PAGE)
    lengths = lengths.at[highest].set(MAXP * PAGE)
    return lengths


def plant(result, key, smallest, high):
    extent = result.shape
    place = [jax.random.randint(jax.random.fold_in(key, axis), (), 0, extent[axis]) for axis in range(len(extent))]
    result = result.at[tuple(place)].set(smallest)
    longest = extent.index(max(extent))
    place[longest] = (place[longest] + 1) % extent[longest]
    return result.at[tuple(place)].set(high)


def steps_of(own_key, extent, cuts, least, high):
    factor_of = 1.0
    for axis_at, parts in cuts:
        steps = jax.random.uniform(jax.random.fold_in(jax.random.fold_in(own_key, 6), axis_at), (parts,), jnp.float32, least / len(cuts), high / len(cuts))
        factor_of = factor_of * jnp.repeat(jnp.exp(steps), extent[axis_at] // parts).reshape((-1,) + (1,) * (len(extent) - 1 - axis_at))
    return factor_of


def deal_out(own_key, own, number, rows, amount, top, reach, lean):
    ranking = jax.random.permutation(own_key, amount)
    heavy_load, usual = portions_of(amount, rows * top, reach, lean, True), portions_of(amount, rows * top, reach, lean, False)
    places = jnp.arange(amount)

    def named(sizes, turn):
        used = int((sizes > 0).sum())
        fixed = max(1, used // 4)
        moved = fixed + (places - fixed + turn * (used - fixed)) % max(1, amount - fixed)
        return jnp.zeros((amount,), jnp.int32).at[ranking[jnp.where(places < fixed, places, moved)]].set(jnp.asarray(sizes, jnp.int32))

    sizes = jnp.where(number % 4 == 0, named(heavy_load, number // 4), named(usual, number - number // 4 - 1))
    mixed = jax.random.permutation(jax.random.fold_in(own, 3), amount)
    source_of, taker = mixed[0:amount // 2 * 2:2], mixed[1:amount // 2 * 2:2]
    margin = jnp.minimum(sizes[source_of] - 1, reach - sizes[taker]) // 2
    margin = jnp.where((source_of == ranking[0]) | (taker == ranking[0]) | (sizes[taker] == 0), 0, jnp.maximum(margin, 0))
    moved = jax.random.randint(jax.random.fold_in(own, 4), (amount // 2,), 0, 1 << 20) % (margin + 1)
    sizes = sizes.at[source_of].add(-moved).at[taker].add(moved)
    items = jnp.searchsorted(jnp.cumsum(sizes), jnp.arange(rows * top), side="right").astype(jnp.int32)
    listing = items.reshape(top, rows).T
    listing = listing[jax.random.permutation(jax.random.fold_in(own, 1), rows)]
    turn = jax.random.randint(jax.random.fold_in(own, 2), (rows, 1), 0, top)
    return jnp.take_along_axis(listing, (jnp.arange(top)[None, :] + turn) % top, axis=1)


def portions_of(amount, total, reach, skew, full):
    loads = [(1 << 20) // math.isqrt(rank ** skew) + 1 for rank in range(1, amount + 1)]
    largest = reach if full else min(reach, max(-(-total // amount), total * loads[0] // sum(loads)))
    least = 1 if total - largest >= amount - 1 else 0
    given, rest = [largest] + [least] * (amount - 1), total - largest - least * (amount - 1)
    while rest > 0:
        movable = [i for i in range(1, amount) if given[i] < largest] or [i for i in range(1, amount) if given[i] < reach]
        whole, budget = sum([loads[i] for i in movable]), rest
        for i in movable:
            more = min(reach - given[i], max(1, budget * loads[i] // whole), rest)
            given[i] = given[i] + more
            rest = rest - more
    return np.array(given)


def scatter_about(own_key, dims, deviation, most, shards=(), held_as=jnp.bfloat16):
    result = jax.random.normal(own_key, dims, jnp.float32) * deviation
    if len(shards) > 0:
        result = steps_of(own_key, dims, shards, -0.22, 0.18) * result
    return jnp.clip(result, min=-most, max=most).astype(held_as)


def setup_inputs(seed: int = 0) -> dict:
    key_list = jax.random.split(jax.random.key(seed), 9)
    tokens = scatter_about(key_list[0], (TOKENS, D), 1.0, 6.0, ((0, 16), (1, 8)))
    w_query = scatter_about(key_list[1], (D, QH * HD), D ** -0.5, 0.0625, ((1, 8),))
    w_key = scatter_about(key_list[2], (D, KVH * HD), D ** -0.5, 0.0625, ((1, 8),))
    w_value = scatter_about(key_list[3], (D, KVH * HD), D ** -0.5, 0.0625, ((1, 8),))
    kv_pool = draw_kv_pool(jax.random.fold_in(key_list[8], 71), 0)
    page_owner_keys = jax.random.split(jax.random.fold_in(key_list[5], 1), NODES * MAXP // (NODES_DEV * MAXP))
    page_owner_turns = jax.random.permutation(jax.random.fold_in(key_list[5], 3), NODES * MAXP // (NODES_DEV * MAXP))
    page_owner = jax.vmap(lambda own, number: deal_out(jax.random.fold_in(key_list[5], 2), own, number, NODES_DEV * MAXP, N_POOL, 1, CAP, 1))(page_owner_keys, page_owner_turns).reshape((NODES, MAXP, 1))
    page_slot = plant(jax.random.randint(key_list[6], (NODES, MAXP), 0, SLOTS), jax.random.fold_in(key_list[6], 1), 0, SLOTS - 1).astype(jnp.int32)
    prefix_len = draw_prefix_len(jax.random.fold_in(key_list[8], 71), 0)
    return dict(tokens=tokens, w_query=w_query, w_key=w_key, w_value=w_value, kv_pool=kv_pool, page_owner=page_owner, page_slot=page_slot, prefix_len=prefix_len)


rope_base = 500000.0
norm_eps = 1e-05

def rotate(values, positions):
    half_dim = values.shape[-1] // 2
    inverse = rope_base ** (-(jnp.arange(half_dim, dtype=jnp.float32) * 2.0 / values.shape[-1]))
    angles = positions[..., None] * inverse
    cosine = jnp.cos(angles)
    sine_part = jnp.sin(angles)
    first_half = values[..., :half_dim]
    second_half = values[..., half_dim:]
    return jnp.concatenate([first_half * cosine - second_half * sine_part, second_half * cosine + first_half * sine_part], axis=-1)

def attend_node(queries, keys_new, values_new, node_pages, length):
    suffix_len, kv_heads, group_size, head_dim = queries.shape
    pages_count, page_len = (node_pages.shape[0], node_pages.shape[3])
    score_scale = head_dim ** (-0.5)
    query_wide = queries.astype(jnp.float32)
    prefix_keys = node_pages[:, :, 0].astype(jnp.float32)
    prefix_vals = node_pages[:, :, 1].astype(jnp.float32)
    prefix_scores = jnp.einsum('skgd,pkjd->kgspj', query_wide, prefix_keys)
    prefix_scores = prefix_scores.reshape(kv_heads, group_size, suffix_len, pages_count * page_len) * score_scale
    key_place = jnp.arange(pages_count * page_len, dtype=jnp.int32)
    prefix_scores = jnp.where(key_place < length, prefix_scores, -jnp.inf)
    own_scores = jnp.einsum('skgd,tkd->kgst', query_wide, keys_new.astype(jnp.float32)) * score_scale
    causal = jnp.arange(suffix_len)[:, None] >= jnp.arange(suffix_len)[None, :]
    own_scores = jnp.where(causal, own_scores, -jnp.inf)
    peak = jnp.maximum(prefix_scores.max(-1), own_scores.max(-1))
    prefix_weights = jnp.exp(prefix_scores - peak[..., None])
    own_weights = jnp.exp(own_scores - peak[..., None])
    weight_sum = prefix_weights.sum(-1) + own_weights.sum(-1)
    prefix_round = lax.optimization_barrier(prefix_weights.astype(jnp.bfloat16)).astype(jnp.float32)
    own_round = lax.optimization_barrier(own_weights.astype(jnp.bfloat16)).astype(jnp.float32)
    prefix_round = prefix_round.reshape(kv_heads, group_size, suffix_len, pages_count, page_len)
    combined = jnp.einsum('kgspj,pkjd->kgsd', prefix_round, prefix_vals)
    combined = combined + jnp.einsum('kgst,tkd->kgsd', own_round, values_new.astype(jnp.float32))
    combined = combined / weight_sum[..., None]
    return jnp.transpose(combined, (2, 0, 1, 3)).reshape(suffix_len, kv_heads * group_size * head_dim).astype(jnp.bfloat16)

def reference(tokens, w_query, w_key, w_value, kv_pool, page_owner, page_slot, prefix_len):
    widened = tokens.astype(jnp.float32)
    normed = (widened * lax.rsqrt(lax.optimization_barrier(jnp.mean(widened * widened, axis=-1, keepdims=True)) + norm_eps)).astype(jnp.bfloat16)
    queries = jnp.dot(normed, w_query, preferred_element_type=jnp.float32).reshape(NODES, SUF, QH, HD)
    keys_new = jnp.dot(normed, w_key, preferred_element_type=jnp.float32).reshape(NODES, SUF, KVH, HD)
    values_new = jnp.dot(normed, w_value, preferred_element_type=jnp.float32).reshape(NODES, SUF, KVH, HD)
    positions = (prefix_len[:, None] + jnp.arange(SUF, dtype=jnp.int32)[None, :]).astype(jnp.float32)[:, :, None]
    queries = rotate(queries, positions).astype(jnp.bfloat16)
    keys_new = rotate(keys_new, positions).astype(jnp.bfloat16)
    values_new = values_new.astype(jnp.bfloat16)
    suffix_kv = jnp.stack([keys_new, values_new], axis=2).reshape(TOKENS, 2, KVH, HD)
    page_index = (page_owner[..., 0] * SLOTS + page_slot).astype(jnp.int32)

    def one_node(node_items):
        node_query, node_keys, node_values, node_table, node_length = node_items
        return attend_node(node_query.reshape(SUF, KVH, QH // KVH, HD), node_keys, node_values, kv_pool[node_table], node_length)
    attended = lax.map(one_node, (queries, keys_new, values_new, page_index, prefix_len))
    return (attended.reshape(TOKENS, QH * HD), suffix_kv)
```

```python
import functools
import math

import jax
import jax.numpy as jnp
from jax import lax
from jax.experimental import pallas as pl
from jax.experimental.pallas import tpu as pltpu
from jax.sharding import PartitionSpec as P

HD = 128
SUF = 64
PAGE = 64
MAXP = 128
NODES = 3
GROUPS = 4
HEADS = 8
ROWS = HEADS * SUF
BLOCK = 8
KEYS = BLOCK * PAGE
FEATURES = 8192

rope_base = 500000.0
norm_eps = 1e-05
FACTOR = math.log2(math.e) / math.sqrt(HD)
LOW = -1e30

AX = ("pool", "tp")
EVERY = [(x, y, z, c) for x in range(4) for y in range(4) for z in range(4) for c in range(2)]


def flat(x, y, z, c):
    return ((x % 4) * 4 + y % 4) * 8 + (z % 4) * 2 + c


def page_shift(s):
    return [(flat(x, y, z, c), flat(x + s * c, y + s * (1 - c), z, c)) for x, y, z, c in EVERY]


def query_shift(s):
    return [(flat(x, y, z, c), flat(x + s * (1 - c), y + s * c, z, c)) for x, y, z, c in EVERY]


def z_shift(s):
    return [(flat(x, y, z, c), flat(x, y, z + s, c)) for x, y, z, c in EVERY]


def core_swap():
    return [(flat(x, y, z, c), flat(x, y, z, 1 - c)) for x, y, z, c in EVERY]


def project_kernel(shape, ranks, *refs):
    refs = list(refs)
    groups = [[refs.pop(0) for _ in range(n)] for n in shape]
    wq, wk, wv, cos, sin, q_out, kv_out, w_s, x_s, sems = refs

    copies = []
    for t in range(4):
        copies.append([pltpu.make_async_copy(wq.at[:, pl.ds(t * 256, 256)], w_s.at[t], sems.at[t])])
    copies.append(
        [
            pltpu.make_async_copy(wk, w_s.at[4, :, pl.ds(0, 128)], sems.at[4]),
            pltpu.make_async_copy(wv, w_s.at[4, :, pl.ds(128, 128)], sems.at[5]),
        ]
    )
    for some in copies:
        for copy in some:
            copy.start()
    load = lambda group: jnp.concatenate([r[...] for r in group], axis=0) if len(group) > 1 else group[0][...]
    total = jnp.zeros((192, 128), jnp.float32)
    for group in groups:
        wide = load(group).astype(jnp.float32)
        for k in range(8):
            part = wide[:, k * 128 : (k + 1) * 128]
            total = total + part * part
    scale = lax.rsqrt(jnp.sum(total, axis=-1, keepdims=True) * (1.0 / FEATURES) + norm_eps)
    for i, group in enumerate(groups):
        x_s[ranks[i]] = (load(group).astype(jnp.float32) * scale).astype(jnp.bfloat16)
    for t, some in enumerate(copies):
        for copy in some:
            copy.wait()
        total = None
        for r in range(8):
            part = jnp.dot(x_s[r], w_s[t, r * 1024 : (r + 1) * 1024, :], preferred_element_type=jnp.float32)
            total = part if total is None else total + part
        for h in range(2):
            u = total[:, h * HD : (h + 1) * HD]
            g = t * 2 + h
            if g <= HEADS:
                u = u * cos[...] + pltpu.roll(u, 64, 1) * sin[...]
            u = u.astype(jnp.bfloat16)
            if g < HEADS:
                q_out[:, g * HD : (g + 1) * HD] = u
            else:
                kv_out[:, (g - HEADS) * HD : (g - HEADS + 1) * HD] = u


def project(xs, ranks, wq, wk, wv, rope):
    shape = tuple(len(g) for g in xs)
    flat_xs = [a for g in xs for a in g]
    vmem = pl.BlockSpec(memory_space=pltpu.VMEM)
    hbm = pl.BlockSpec(memory_space=pltpu.HBM)
    outs = [jax.ShapeDtypeStruct((192, 1024), jnp.bfloat16), jax.ShapeDtypeStruct((192, 256), jnp.bfloat16)]
    return pl.pallas_call(
        functools.partial(project_kernel, shape),
        out_shape=outs,
        in_specs=[pl.BlockSpec(memory_space=pltpu.SMEM)] + [vmem] * len(flat_xs) + [hbm] * 3 + [vmem] * 2,
        out_specs=[vmem] * 2,
        scratch_shapes=[
            pltpu.VMEM((5, FEATURES, 256), jnp.bfloat16),
            pltpu.VMEM((8, 192, 1024), jnp.bfloat16),
            pltpu.SemaphoreType.DMA((6,)),
        ],
        compiler_params=pltpu.CompilerParams(vmem_limit_bytes=48 * 2**20),
        cost_estimate=pl.CostEstimate(flops=10**6, bytes_accessed=10**6, transcendentals=0),
    )(jnp.stack(ranks).astype(jnp.int32), *flat_xs, wq, wk, wv, *rope)


def attend_kernel(groups, plan, idx, steps, keys, *refs):
    refs = list(refs)
    take = lambda n: [refs.pop(0) for _ in range(n)]
    pages = take(len(plan))
    qs = take(len(groups))
    own = groups == (3,)
    suffix = take(1)[0] if own else None
    outs = [take(2 if own else 1) for _ in groups]
    pool, q_s, s_s, mx_s, acc_s, sems = refs

    copies = []
    for i, (at, ref) in enumerate(zip(plan, pages)):
        copies.append(pltpu.make_async_copy(ref.at[:, 0], pool.at[pl.ds(at, ref.shape[0])], sems.at[i]))
    for copy in copies:
        copy.start()
    for k, q in enumerate(qs):
        for n in range(NODES):
            for g in range(HEADS):
                q_s[k * NODES + n, g * SUF : (g + 1) * SUF, :] = q[n * SUF : (n + 1) * SUF, g * HD : (g + 1) * HD]
    for copy in copies:
        copy.wait()

    lane = lax.broadcasted_iota(jnp.int32, (1, KEYS), 1)
    ones = jnp.ones((KEYS, HD), jnp.bfloat16)

    def node(n, _):
        row = n + groups[0] * NODES
        mx_s[...] = jnp.full_like(mx_s, LOW)
        limit = keys[row]

        def scores(i, _):
            k = jnp.concatenate([pool[idx[row, i * BLOCK + u], 0] for u in range(BLOCK)], axis=0)
            s = lax.dot_general(q_s[n], k, (((1,), (1,)), ((), ())), preferred_element_type=jnp.float32)
            s = s + jnp.where(lane + i * KEYS < limit, 0.0, LOW)
            s_s[i] = s
            top = mx_s[...]
            for u in range(KEYS // 128):
                top = jnp.maximum(top, s[:, u * 128 : (u + 1) * 128])
            mx_s[...] = top
            return 0

        lax.fori_loop(0, steps[row], scores, 0)
        peak = jnp.max(mx_s[...], axis=-1, keepdims=True)
        if own:
            local = n
            r = pl.ds(pl.multiple_of(local * SUF, SUF), SUF)
            s_new = lax.dot_general(q_s[n], suffix[r, :HD], (((1,), (1,)), ((), ())), preferred_element_type=jnp.float32)
            i = lax.broadcasted_iota(jnp.int32, (ROWS, SUF), 0) % SUF
            j = lax.broadcasted_iota(jnp.int32, (ROWS, SUF), 1)
            s_new = jnp.where(j <= i, s_new, LOW)
            peak = jnp.maximum(jnp.max(s_new, axis=-1, keepdims=True), peak)
        shift = peak * FACTOR
        if own:
            w = jnp.exp2(s_new * FACTOR - shift).astype(jnp.bfloat16)
            v = jnp.concatenate([suffix[r, HD:], ones[:SUF]], axis=1)
            acc_s[...] = jnp.dot(w, v, preferred_element_type=jnp.float32)
        else:
            acc_s[...] = jnp.zeros_like(acc_s)

        def values(i, _):
            v = jnp.concatenate([pool[idx[row, i * BLOCK + u], 1] for u in range(BLOCK)], axis=0)
            w = jnp.exp2(s_s[i] * FACTOR - shift).astype(jnp.bfloat16)
            acc_s[...] += jnp.dot(w, jnp.concatenate([v, ones], axis=1), preferred_element_type=jnp.float32)
            return 0

        lax.fori_loop(0, steps[row], values, 0)

        at = lax.broadcasted_iota(jnp.int32, (SUF, 128), 1)
        total = jnp.ones((SUF, 128), jnp.float32)
        level = jnp.full((SUF, 128), LOW, jnp.float32)
        for g in range(HEADS):
            rows = slice(g * SUF, (g + 1) * SUF)
            total = jnp.where(at == g, acc_s[rows, HD:], total)
            level = jnp.where(at == g, shift[rows], level)
        some = total > 0.0
        total = jnp.where(some, total, 1.0)
        level = jnp.where(some, level + jnp.log2(total), LOW)
        share = jnp.where(some, 1.0 / total, 0.0)
        if not own:
            tile = jnp.where(at < HEADS, level, 0.0)
            high = tile.astype(jnp.bfloat16).astype(jnp.float32)
            rest = tile - high
            mid = rest.astype(jnp.bfloat16).astype(jnp.float32)
            level = high + pltpu.roll(mid, 8, 1) + pltpu.roll(rest - mid, 16, 1)

        def put(out, local):
            r = pl.ds(pl.multiple_of(local * SUF, SUF), SUF)
            for g in range(HEADS):
                o = acc_s[g * SUF : (g + 1) * SUF, :HD] * share[:, g : g + 1]
                out[0][r, g * HD : (g + 1) * HD] = o.astype(out[0].dtype)
            if own:
                out[1][r, :] = level
            else:
                out[0][r, HEADS * HD :] = level.astype(jnp.bfloat16)

        for k in range(len(groups)):

            @pl.when((n >= k * NODES) & (n < (k + 1) * NODES))
            def _():
                put(outs[k], n - k * NODES)

        return 0

    lax.fori_loop(0, len(groups) * NODES, node, 0)


def attend(groups, lists, pages, qs, suffix):
    own = groups == (3,)
    f32 = jnp.float32
    if own:
        outs = [jax.ShapeDtypeStruct((192, 1024), f32), jax.ShapeDtypeStruct((192, 128), f32)]
    else:
        outs = [jax.ShapeDtypeStruct((192, 1152), jnp.bfloat16) for _ in groups]
    n = len(groups) * NODES
    extra = [suffix] if own else []
    vmem = pl.BlockSpec(memory_space=pltpu.VMEM)
    smem = pl.BlockSpec(memory_space=pltpu.SMEM)
    hbm = pl.BlockSpec(memory_space=pl.ANY)
    return pl.pallas_call(
        functools.partial(attend_kernel, groups, tuple(at for at, _ in pages)),
        out_shape=outs,
        in_specs=[smem] * 3 + [hbm] * len(pages) + [vmem] * (len(qs) + len(extra)),
        out_specs=[vmem] * len(outs),
        scratch_shapes=[
            pltpu.VMEM((sum(a.shape[0] for _, a in pages), 2, PAGE, HD), jnp.bfloat16),
            pltpu.VMEM((n, ROWS, HD), jnp.bfloat16),
            pltpu.VMEM((MAXP // BLOCK, ROWS, KEYS), f32),
            pltpu.VMEM((ROWS, 128), f32),
            pltpu.VMEM((ROWS, 2 * HD), f32),
            pltpu.SemaphoreType.DMA((len(pages),)),
        ],
        compiler_params=pltpu.CompilerParams(vmem_limit_bytes=36 * 2**20),
        cost_estimate=pl.CostEstimate(flops=10**9, bytes_accessed=10**6, transcendentals=0),
    )(*lists, *[a for _, a in pages], *qs, *extra)


def merge_kernel(o_ref, l_ref, a_ref, b_ref, c_ref, out_ref):
    others = [a_ref, b_ref, c_ref]
    levels = [l_ref[...]]
    for r in others:
        t = r[:, HEADS * HD :].astype(jnp.float32)
        levels.append(t + pltpu.roll(t, 120, 1) + pltpu.roll(t, 112, 1))
    top = functools.reduce(jnp.maximum, levels)
    weights = [jnp.exp2(v - top) for v in levels]
    share = 1.0 / functools.reduce(jnp.add, weights)
    weights = [w * share for w in weights]
    for g in range(HEADS):
        cols = slice(g * HD, (g + 1) * HD)
        out = o_ref[:, cols] * weights[0][:, g : g + 1]
        for w, r in zip(weights[1:], others):
            out = out + r[:, cols].astype(jnp.float32) * w[:, g : g + 1]
        out_ref[:, cols] = out.astype(jnp.bfloat16)


def make_lists(mask, where, lens):
    place = jnp.arange(MAXP, dtype=jnp.int32)
    upto = jnp.sum(jnp.where(place[None, None, :] <= place[None, :, None], mask[:, None, :], False).astype(jnp.int32), axis=-1)
    hit = mask[:, None, :] & (upto[:, None, :] - 1 == place[None, :, None])
    idx = jnp.sum(jnp.where(hit, where[:, None, :], 0), axis=-1)
    count = jnp.sum(mask.astype(jnp.int32), axis=-1)
    keys = jnp.sum(jnp.where(mask, jnp.minimum(PAGE, lens[:, None] - place[None, :] * PAGE), 0), axis=-1)
    return idx, (count + BLOCK - 1) // BLOCK, keys


def body(tokens, w_query, w_key, w_value, kv_pool, page_owner, page_slot, prefix_len):
    pool_at, tp_at = lax.axis_index("pool"), lax.axis_index("tp")
    x, y, core = pool_at // 4, pool_at % 4, tp_at % 2
    along_page = jnp.where(core == 0, y, x)
    along_query = jnp.where(core == 0, x, y)
    move = lambda a, perm: lax.ppermute(a, AX, perm)

    tok_a, tok_b = move(tokens, z_shift(1)), move(tokens, z_shift(-1))
    tok_o = move(tokens, core_swap())
    page_a, page_b = move(kv_pool, page_shift(1)), move(kv_pool, page_shift(-1))
    positions = (prefix_len[:, None] + jnp.arange(SUF, dtype=jnp.int32)[None, :]).astype(jnp.float32).reshape(192, 1)
    inverse = rope_base ** (-(jnp.arange(HD // 2, dtype=jnp.float32) * 2.0 / HD))
    angles = positions * inverse
    cosine, sine = jnp.cos(angles), jnp.sin(angles)
    rope = (jnp.concatenate([cosine, cosine], axis=1), jnp.concatenate([-sine, sine], axis=1))

    tok_ao, tok_bo = move(tok_a, core_swap()), move(tok_b, core_swap())
    tok_c, tok_d = move(tok_a[:96], z_shift(1)), move(tok_b[96:], z_shift(-1))
    tok_co, tok_do = move(tok_c, core_swap()), move(tok_d, core_swap())

    table = jnp.concatenate(
        [page_owner[..., 0] * 64 + page_slot, jnp.broadcast_to(jnp.pad(prefix_len, (0, MAXP - NODES))[None], (1, MAXP))], axis=0
    )
    table = lax.optimization_barrier((table, tok_a, tok_b))[0]
    tables = [move(table, query_shift(-1)), move(table, query_shift(1)), move(table, query_shift(2)), table]

    page_a, page_b, tok_co, tok_do = lax.optimization_barrier((page_a, page_b, tok_co, tok_do))
    page_c, page_d = move(page_a[:32], page_shift(1)), move(page_b[32:], page_shift(-1))
    z = tp_at // 2
    rank = lambda dz, same: ((z + dz) % 4) * 2 + (core if same else 1 - core)
    blocks = [[tokens], [tok_o], [tok_a], [tok_b], [tok_ao], [tok_bo], [tok_c, tok_d], [tok_co, tok_do]]
    ranks = [rank(dz, same) for dz, same in ((0, 1), (0, 0), (-1, 1), (1, 1), (-1, 0), (1, 0), (2, 1), (2, 0))]
    queries, suffix = project(blocks, ranks, w_query, w_key, w_value, rope)
    suffix_kv = suffix.reshape(192, 2, 1, HD)

    qs = [move(queries, query_shift(-1)), move(queries, query_shift(1)), move(queries, query_shift(2))]

    pages = ((0, kv_pool), (64, page_a), (128, page_b), (192, page_c), (224, page_d))
    codes = jnp.concatenate([t[:NODES] for t in tables], axis=0)
    lens = jnp.concatenate([t[NODES, :NODES] for t in tables], axis=0)
    owner, slot = codes // 64, codes % 64
    owner_page = jnp.where(core == 0, owner % 4, owner // 4)
    owner_query = jnp.where(core == 0, owner // 4, owner % 4)
    apart = (owner_page - along_page) % 4
    needed = (owner_query == along_query) & (jnp.arange(MAXP, dtype=jnp.int32)[None, :] * PAGE < lens[:, None])
    start = jnp.where(apart == 0, 0, jnp.where(apart == 3, 64, jnp.where(apart == 1, 128, 192)))
    lists = make_lists(needed, start + slot, lens)
    sent = attend((0, 1, 2), lists, pages, qs, None)
    back = [move(r, query_shift(s)) for r, s in zip(sent, (1, -1, 2))]
    mine = attend((3,), lists, pages, [queries], suffix)
    attended = pl.pallas_call(
        merge_kernel,
        out_shape=jax.ShapeDtypeStruct((192, 1024), jnp.bfloat16),
        compiler_params=pltpu.CompilerParams(vmem_limit_bytes=16 * 2**20),
    )(*mine, *back)
    return attended, suffix_kv


def solution(mesh):
    in_specs = (
        P("pool", "tp"),
        P(None, "tp"),
        P(None, "tp"),
        P(None, "tp"),
        P("pool", "tp", None, None, None),
        P("pool", None, None),
        P("pool", None),
        P("pool"),
    )
    out_specs = (P("pool", "tp"), P("pool", None, "tp", None))
    return jax.shard_map(body, mesh=mesh, in_specs=in_specs, out_specs=out_specs, check_vma=False)
```

```python
import functools
import math

import jax
import jax.numpy as jnp
from jax import lax
from jax.experimental import pallas as pl
from jax.experimental.pallas import tpu as pltpu
from jax.sharding import PartitionSpec as P

HD = 128
SUF = 64
PAGE = 64
MAXP = 128
NODES = 3
GROUPS = 4
HEADS = 8
ROWS = HEADS * SUF
BLOCK = 8
KEYS = BLOCK * PAGE
FEATURES = 8192

rope_base = 500000.0
norm_eps = 1e-05
FACTOR = math.log2(math.e) / math.sqrt(HD)
LOW = -1e30

AX = ("pool", "tp")
EVERY = [(x, y, z, c) for x in range(4) for y in range(4) for z in range(4) for c in range(2)]


def flat(x, y, z, c):
    return ((x % 4) * 4 + y % 4) * 8 + (z % 4) * 2 + c


def page_shift(s):
    return [(flat(x, y, z, c), flat(x + s * c, y + s * (1 - c), z, c)) for x, y, z, c in EVERY]


def query_shift(s):
    return [(flat(x, y, z, c), flat(x + s * (1 - c), y + s * c, z, c)) for x, y, z, c in EVERY]


def z_shift(s):
    return [(flat(x, y, z, c), flat(x, y, z + s, c)) for x, y, z, c in EVERY]


def core_swap():
    return [(flat(x, y, z, c), flat(x, y, z, 1 - c)) for x, y, z, c in EVERY]


def project_kernel(shape, ranks, *refs):
    refs = list(refs)
    xs = [[refs.pop(0) for _ in range(n)] for n in shape]
    load = lambda group: jnp.concatenate([r[...] for r in group], axis=0).astype(jnp.float32)
    (wq, wk, wv, cos, sin, tails), refs = refs[:6], refs[6:]
    sends, (q_out, kv_out, w_s, x_s, sems) = refs[:3], refs[3:]

    copies = []
    for t in range(4):
        copies.append([pltpu.make_async_copy(wq.at[:, pl.ds(t * 256, 256)], w_s.at[t], sems.at[t])])
    copies.append(
        [
            pltpu.make_async_copy(wk, w_s.at[4, :, pl.ds(0, 128)], sems.at[4]),
            pltpu.make_async_copy(wv, w_s.at[4, :, pl.ds(128, 128)], sems.at[5]),
        ]
    )
    for some in copies:
        for copy in some:
            copy.start()
    for k, send in enumerate(sends):
        send[:, HD:] = tails[k]
    total = jnp.zeros((192, 128), jnp.float32)
    for x in xs:
        wide = load(x)
        for k in range(8):
            part = wide[:, k * 128 : (k + 1) * 128]
            total = total + part * part
    scale = lax.rsqrt(jnp.sum(total, axis=-1, keepdims=True) * (1.0 / FEATURES) + norm_eps)
    for i, x in enumerate(xs):
        x_s[ranks[i]] = (load(x) * scale).astype(jnp.bfloat16)
    for t, some in enumerate(copies):
        for copy in some:
            copy.wait()
        total = None
        for r in range(8):
            part = jnp.dot(x_s[r], w_s[t, r * 1024 : (r + 1) * 1024, :], preferred_element_type=jnp.float32)
            total = part if total is None else total + part
        turned = []
        for h in range(2):
            u = total[:, h * HD : (h + 1) * HD]
            g = t * 2 + h
            if g <= HEADS:
                u = u * cos[...] + pltpu.roll(u, 64, 1) * sin[...]
            if g < HEADS:
                turned.append(u)
            else:
                kv_out[:, (g - HEADS) * HD : (g - HEADS + 1) * HD] = u.astype(jnp.bfloat16)
        if turned:
            for n in range(NODES):
                both = jnp.concatenate([u[n * SUF : (n + 1) * SUF] for u in turned], axis=0).T.astype(jnp.bfloat16)
                q_out[n, :, t * 128 : (t + 1) * 128] = both
                for send in sends:
                    send[n, :HD, t * 128 : (t + 1) * 128] = both


def project(xs, ranks, wq, wk, wv, rope, tails):
    vmem = pl.BlockSpec(memory_space=pltpu.VMEM)
    hbm = pl.BlockSpec(memory_space=pltpu.HBM)
    bf16 = jnp.bfloat16
    outs = [jax.ShapeDtypeStruct((NODES, HD + 16, ROWS), bf16)] * 3
    outs += [jax.ShapeDtypeStruct((NODES, HD, ROWS), bf16), jax.ShapeDtypeStruct((192, 256), bf16)]
    shape = tuple(len(g) for g in xs)
    xs = [a for g in xs for a in g]
    return pl.pallas_call(
        functools.partial(project_kernel, shape),
        out_shape=outs,
        in_specs=[pl.BlockSpec(memory_space=pltpu.SMEM)] + [vmem] * len(xs) + [hbm] * 3 + [vmem] * 3,
        out_specs=[vmem] * 5,
        scratch_shapes=[
            pltpu.VMEM((5, FEATURES, 256), bf16),
            pltpu.VMEM((8, 192, 1024), bf16),
            pltpu.SemaphoreType.DMA((6,)),
        ],
        compiler_params=pltpu.CompilerParams(vmem_limit_bytes=48 * 2**20),
        cost_estimate=pl.CostEstimate(flops=10**6, bytes_accessed=10**6, transcendentals=0),
    )(jnp.stack(ranks).astype(jnp.int32), *xs, wq, wk, wv, *rope, tails)


def attend_kernel(groups, plan, idx, steps, keys, *refs):
    refs = list(refs)
    take = lambda n: [refs.pop(0) for _ in range(n)]
    pages = take(len(plan))
    qs = take(len(groups))
    own = groups == (3,)
    suffix = take(1)[0] if own else None
    outs = [take(2 if own else 1) for _ in groups]
    pool, q_s, s_a, s_b, acc_s, sems = refs

    copies = []
    for i, (at, ref) in enumerate(zip(plan, pages)):
        copies.append(pltpu.make_async_copy(ref.at[:, 0], pool.at[pl.ds(at, ref.shape[0])], sems.at[i]))
    for copy in copies:
        copy.start()
    for k, q in enumerate(qs):
        q_s[k * NODES : (k + 1) * NODES] = q[:, :HD]
    for copy in copies:
        copy.wait()

    place = lax.broadcasted_iota(jnp.int32, (PAGE, 1), 0)
    over_keys = (((0,), (0,)), ((), ()))
    nodes = len(groups) * NODES

    def scores(n, i, s_ref):
        k = jnp.concatenate([pool[idx[n, i * BLOCK + u], 0] for u in range(BLOCK)], axis=0)
        s_ref[...] = jnp.dot(k, q_s[n], preferred_element_type=jnp.float32)

    def mask(n, i, s_ref):
        left = keys[n] - i * KEYS
        for u in range(BLOCK):

            @pl.when(left < (u + 1) * PAGE)
            def _():
                rows = slice(u * PAGE, (u + 1) * PAGE)
                s_ref[rows] = jnp.where(place < left - u * PAGE, s_ref[rows], LOW)

    def values(n, i, s_ref, peak, total):
        v = jnp.concatenate([pool[idx[n, i * BLOCK + u], 1] for u in range(BLOCK)], axis=0)
        s = s_ref[...]
        old = jnp.where(i == 0, LOW, peak)
        peak = jnp.maximum(old, jnp.max(jnp.max(s.reshape(-1, 8, ROWS), axis=0), axis=0, keepdims=True))
        keep = jnp.exp2((old - peak) * FACTOR)
        w = jnp.exp2(s * FACTOR - peak * FACTOR)
        total = total * keep + jnp.sum(w.reshape(-1, 8, ROWS), axis=0)
        acc_s[...] = acc_s[...] * keep + lax.dot_general(
            v, w.astype(jnp.bfloat16), over_keys, preferred_element_type=jnp.float32
        )
        return peak, total

    def finish(n, peak, total):
        total = jnp.sum(total, axis=0, keepdims=True)
        out = acc_s[...]
        if own:
            r = pl.ds(pl.multiple_of(n * SUF, SUF), SUF)
            s = jnp.dot(suffix[r, :HD], q_s[n], preferred_element_type=jnp.float32)
            key = lax.broadcasted_iota(jnp.int32, (SUF, ROWS), 0)
            query = lax.broadcasted_iota(jnp.int32, (SUF, ROWS), 1) % SUF
            s = jnp.where(key <= query, s, LOW)
            old = peak
            peak = jnp.maximum(jnp.max(s, axis=0, keepdims=True), old)
            keep = jnp.exp2((old - peak) * FACTOR)
            w = jnp.exp2((s - peak) * FACTOR)
            new = lax.dot_general(suffix[r, HD:], w.astype(jnp.bfloat16), over_keys, preferred_element_type=jnp.float32)
            out = out * keep + new
            total = total * keep + jnp.sum(w, axis=0, keepdims=True)
        level = peak * FACTOR + jnp.log2(total)
        out = out * (1.0 / total)
        if own:
            outs[0][0][n] = out
            outs[0][1][n] = jnp.broadcast_to(level, (8, ROWS))
        else:
            high = level.astype(jnp.bfloat16).astype(jnp.float32)
            rest = level - high
            mid = rest.astype(jnp.bfloat16).astype(jnp.float32)
            at = lax.broadcasted_iota(jnp.int32, (16, ROWS), 0)
            tile = jnp.where(at == 0, high, jnp.where(at == 1, mid, jnp.where(at == 2, rest - mid, 0.0)))
            for k in range(len(groups)):

                @pl.when((n >= k * NODES) & (n < (k + 1) * NODES))
                def _():
                    outs[k][0][n - k * NODES, :HD] = out.astype(jnp.bfloat16)
                    outs[k][0][n - k * NODES, HD:] = tile.astype(jnp.bfloat16)

    def after(n, i):
        more = (i + 1 < steps[n]) | (n == nodes - 1)
        return jnp.where(more, n, n + 1), jnp.where(more, i + 1, 0)

    def one(n, i, now, later, peak, total):
        n_next, i_next = after(n, i)
        scores(n_next, jnp.minimum(i_next, MAXP // BLOCK - 1), later)
        peak, total = values(n, jnp.minimum(i, MAXP // BLOCK - 1), now, peak, total)

        @pl.when(i == steps[n] - 1)
        def _():
            finish(n, peak, total)

        @pl.when(i_next >= steps[n_next] - 1)
        def _():
            mask(n_next, i_next, later)

        return n_next, i_next, peak, total

    def two(_, state):
        n, i, peak, total = state
        n, i, peak, total = one(n, i, s_a, s_b, peak, total)
        return one(n, i, s_b, s_a, peak, total)

    acc_s[...] = jnp.zeros_like(acc_s)
    scores(0, 0, s_a)
    mask(0, 0, s_a)
    count = lax.fori_loop(0, nodes, lambda n, c: c + steps[n], 0)
    zero = jnp.int32(0)
    lax.fori_loop(
        0, (count + 1) // 2, two, (zero, zero, jnp.full((1, ROWS), LOW, jnp.float32), jnp.zeros((8, ROWS), jnp.float32))
    )


def attend(groups, lists, pages, qs, suffix):
    own = groups == (3,)
    f32 = jnp.float32
    if own:
        outs = [jax.ShapeDtypeStruct((NODES, HD, ROWS), f32), jax.ShapeDtypeStruct((NODES, 8, ROWS), f32)]
    else:
        outs = [jax.ShapeDtypeStruct((NODES, HD + 16, ROWS), jnp.bfloat16) for _ in groups]
    n = len(groups) * NODES
    extra = [suffix] if own else []
    vmem = pl.BlockSpec(memory_space=pltpu.VMEM)
    smem = pl.BlockSpec(memory_space=pltpu.SMEM)
    hbm = pl.BlockSpec(memory_space=pl.ANY)
    return pl.pallas_call(
        functools.partial(attend_kernel, groups, tuple(at for at, _ in pages)),
        out_shape=outs,
        in_specs=[smem] * 3 + [hbm] * len(pages) + [vmem] * (len(qs) + len(extra)),
        out_specs=[vmem] * len(outs),
        scratch_shapes=[
            pltpu.VMEM((sum(a.shape[0] for _, a in pages), 2, PAGE, HD), jnp.bfloat16),
            pltpu.VMEM((n, HD, ROWS), jnp.bfloat16),
            pltpu.VMEM((KEYS, ROWS), f32),
            pltpu.VMEM((KEYS, ROWS), f32),
            pltpu.VMEM((HD, ROWS), f32),
            pltpu.SemaphoreType.DMA((len(pages),)),
        ],
        compiler_params=pltpu.CompilerParams(vmem_limit_bytes=(52 if own else 36) * 2**20),
        cost_estimate=pl.CostEstimate(flops=10**9, bytes_accessed=10**6, transcendentals=0),
    )(*lists, *[a for _, a in pages], *qs, *extra)


def merge_kernel(o_ref, l_ref, a_ref, b_ref, c_ref, out_ref):
    others = [a_ref, b_ref, c_ref]
    for n in range(NODES):
        levels = [l_ref[n, :1]]
        for r in others:
            t = r[n, HD:].astype(jnp.float32)
            levels.append(t[0:1] + t[1:2] + t[2:3])
        top = functools.reduce(jnp.maximum, levels)
        weights = [jnp.exp2(v - top) for v in levels]
        share = 1.0 / functools.reduce(jnp.add, weights)
        out = o_ref[n] * (weights[0] * share)
        for w, r in zip(weights[1:], others):
            out = out + r[n, :HD].astype(jnp.float32) * (w * share)
        rows = slice(n * SUF, (n + 1) * SUF)
        for t in range(HEADS // 2):
            both = out[:, t * 128 : (t + 1) * 128].T.astype(jnp.bfloat16)
            out_ref[rows, 2 * t * HD : (2 * t + 1) * HD] = both[:SUF]
            out_ref[rows, (2 * t + 1) * HD : (2 * t + 2) * HD] = both[SUF:]


def make_lists(mask, where, lens):
    place = jnp.arange(MAXP, dtype=jnp.int32)
    upto = jnp.sum(jnp.where(place[None, None, :] <= place[None, :, None], mask[:, None, :], False).astype(jnp.int32), axis=-1)
    hit = mask[:, None, :] & (upto[:, None, :] - 1 == place[None, :, None])
    idx = jnp.sum(jnp.where(hit, where[:, None, :], 0), axis=-1)
    count = jnp.sum(mask.astype(jnp.int32), axis=-1)
    keys = jnp.sum(jnp.where(mask, jnp.minimum(PAGE, lens[:, None] - place[None, :] * PAGE), 0), axis=-1)
    return idx, jnp.maximum((count + BLOCK - 1) // BLOCK, 1), keys


def body(tokens, w_query, w_key, w_value, kv_pool, page_owner, page_slot, prefix_len):
    pool_at, tp_at = lax.axis_index("pool"), lax.axis_index("tp")
    x, y, core = pool_at // 4, pool_at % 4, tp_at % 2
    along_page = jnp.where(core == 0, y, x)
    along_query = jnp.where(core == 0, x, y)
    move = lambda a, perm: lax.ppermute(a, AX, perm)

    tok_a, tok_b = move(tokens, z_shift(1)), move(tokens, z_shift(-1))
    tok_o = move(tokens, core_swap())
    page_a, page_b = move(kv_pool, page_shift(1)), move(kv_pool, page_shift(-1))

    positions = (prefix_len[:, None] + jnp.arange(SUF, dtype=jnp.int32)[None, :]).astype(jnp.float32).reshape(192, 1)
    inverse = rope_base ** (-(jnp.arange(HD // 2, dtype=jnp.float32) * 2.0 / HD))
    angles = positions * inverse
    cosine, sine = jnp.cos(angles), jnp.sin(angles)
    rope = (jnp.concatenate([cosine, cosine], axis=1), jnp.concatenate([-sine, sine], axis=1))

    owner = page_owner[..., 0]
    owner_page = jnp.where(core == 0, owner % 4, owner // 4)
    owner_query = jnp.where(core == 0, owner // 4, owner % 4)
    apart = (owner_page - along_page) % 4
    start = jnp.where(apart == 0, 0, jnp.where(apart == 3, 64, jnp.where(apart == 1, 128, 192)))
    valid = jnp.arange(MAXP, dtype=jnp.int32)[None, :] * PAGE < prefix_len[:, None]
    masks = jnp.concatenate([valid & (owner_query == (along_query + d) % 4) for d in (1, -1, 2, 0)], axis=0)
    idx, steps, keys = make_lists(masks, jnp.tile(start + page_slot, (4, 1)), jnp.tile(prefix_len, 4))
    numbers = jnp.stack([steps, keys // 64, keys % 64], axis=-1)
    tails = jnp.zeros((9, 16, ROWS), jnp.bfloat16)
    tails = tails.at[:, 0, :MAXP].set(idx[:9].astype(jnp.bfloat16)).at[:, 1, :3].set(numbers[:9].astype(jnp.bfloat16))
    tails = tails.reshape(3, NODES, 16, ROWS)

    tok_a, tok_b, tails, rope = lax.optimization_barrier((tok_a, tok_b, tails, rope))
    tok_ao, tok_bo = move(tok_a, core_swap()), move(tok_b, core_swap())
    tok_c, tok_d = move(tok_a[:96], z_shift(1)), move(tok_b[96:], z_shift(-1))
    tok_co, tok_do = move(tok_c, core_swap()), move(tok_d, core_swap())
    z = tp_at // 2
    rank = lambda dz, same: ((z + dz) % 4) * 2 + (core if same else 1 - core)
    blocks = [[tokens], [tok_o], [tok_a], [tok_b], [tok_ao], [tok_bo], [tok_c, tok_d], [tok_co, tok_do]]
    ranks = [rank(dz, same) for dz, same in ((0, 1), (0, 0), (-1, 1), (1, 1), (-1, 0), (1, 0), (2, 1), (2, 0))]
    *sends, queries, suffix = project(blocks, ranks, w_query, w_key, w_value, rope, tails)
    suffix_kv = suffix.reshape(192, 2, 1, HD)

    page_a, page_b, suffix = lax.optimization_barrier((page_a, page_b, suffix))
    page_c, page_d = move(page_a[:32], page_shift(1)), move(page_b[32:], page_shift(-1))
    qs = [move(sends[1], query_shift(-1)), move(sends[0], query_shift(1)), move(sends[2], query_shift(2))]
    got = jnp.concatenate([q[:, HD : HD + 2, :MAXP] for q in qs], axis=0).astype(jnp.int32)
    theirs = (got[:, 0], got[:, 1, 0], got[:, 1, 1] * 64 + got[:, 1, 2])
    pages = ((0, kv_pool), (64, page_a), (128, page_b), (192, page_c), (224, page_d))
    sent = attend((0, 1, 2), theirs, pages, qs, None)
    back = [move(r, query_shift(s)) for r, s in zip(sent, (1, -1, 2))]
    mine = attend((3,), (idx[9:], steps[9:], keys[9:]), pages, [queries], suffix)
    attended = pl.pallas_call(
        merge_kernel,
        out_shape=jax.ShapeDtypeStruct((192, 1024), jnp.bfloat16),
        compiler_params=pltpu.CompilerParams(vmem_limit_bytes=16 * 2**20),
    )(*mine, *back)
    return attended, suffix_kv


def solution(mesh):
    in_specs = (
        P("pool", "tp"),
        P(None, "tp"),
        P(None, "tp"),
        P(None, "tp"),
        P("pool", "tp", None, None, None),
        P("pool", None, None),
        P("pool", None),
        P("pool"),
    )
    out_specs = (P("pool", "tp"), P("pool", None, "tp", None))
    return jax.shard_map(body, mesh=mesh, in_specs=in_specs, out_specs=out_specs, check_vma=False)
```

```python
import functools
import math

import jax
import jax.numpy as jnp
from jax import lax
from jax.experimental import pallas as pl
from jax.experimental.pallas import tpu as pltpu
from jax.sharding import PartitionSpec as P

HD = 128
SUF = 64
PAGE = 64
MAXP = 128
NODES = 3
GROUPS = 4
HEADS = 8
ROWS = HEADS * SUF
BLOCK = 8
KEYS = BLOCK * PAGE
FEATURES = 8192

rope_base = 500000.0
norm_eps = 1e-05
FACTOR = math.log2(math.e) / math.sqrt(HD)
LOW = -1e30

AX = ("pool", "tp")
EVERY = [(x, y, z, c) for x in range(4) for y in range(4) for z in range(4) for c in range(2)]


def flat(x, y, z, c):
    return ((x % 4) * 4 + y % 4) * 8 + (z % 4) * 2 + c


def page_shift(s):
    return [(flat(x, y, z, c), flat(x + s * c, y + s * (1 - c), z, c)) for x, y, z, c in EVERY]


def query_shift(s):
    return [(flat(x, y, z, c), flat(x + s * (1 - c), y + s * c, z, c)) for x, y, z, c in EVERY]


def z_shift(s):
    return [(flat(x, y, z, c), flat(x, y, z + s, c)) for x, y, z, c in EVERY]


def core_swap():
    return [(flat(x, y, z, c), flat(x, y, z, 1 - c)) for x, y, z, c in EVERY]


def project_kernel(shape, ranks, *refs):
    refs = list(refs)
    xs = [[refs.pop(0) for _ in range(n)] for n in shape]
    load = lambda group: jnp.concatenate([r[...] for r in group], axis=0).astype(jnp.float32)
    (wq, wk, wv, cos, sin, tails), refs = refs[:6], refs[6:]
    sends, (q_out, kv_out, w_s, x_s, sems) = refs[:3], refs[3:]

    copies = []
    for t in range(4):
        copies.append([pltpu.make_async_copy(wq.at[:, pl.ds(t * 256, 256)], w_s.at[t], sems.at[t])])
    copies.append(
        [
            pltpu.make_async_copy(wk, w_s.at[4, :, pl.ds(0, 128)], sems.at[4]),
            pltpu.make_async_copy(wv, w_s.at[4, :, pl.ds(128, 128)], sems.at[5]),
        ]
    )
    for some in copies:
        for copy in some:
            copy.start()
    for k, send in enumerate(sends):
        send[:, HD:] = tails[k]
    total = jnp.zeros((192, 128), jnp.float32)
    for x in xs:
        wide = load(x)
        for k in range(8):
            part = wide[:, k * 128 : (k + 1) * 128]
            total = total + part * part
    scale = lax.rsqrt(jnp.sum(total, axis=-1, keepdims=True) * (1.0 / FEATURES) + norm_eps)
    for i, x in enumerate(xs):
        x_s[ranks[i]] = (load(x) * scale).astype(jnp.bfloat16)
    for t, some in enumerate(copies):
        for copy in some:
            copy.wait()
        total = None
        for r in range(8):
            part = jnp.dot(x_s[r], w_s[t, r * 1024 : (r + 1) * 1024, :], preferred_element_type=jnp.float32)
            total = part if total is None else total + part
        turned = []
        for h in range(2):
            u = total[:, h * HD : (h + 1) * HD]
            g = t * 2 + h
            if g <= HEADS:
                u = u * cos[...] + pltpu.roll(u, 64, 1) * sin[...]
            if g < HEADS:
                turned.append(u)
            else:
                kv_out[:, (g - HEADS) * HD : (g - HEADS + 1) * HD] = u.astype(jnp.bfloat16)
        if turned:
            for n in range(NODES):
                both = jnp.concatenate([u[n * SUF : (n + 1) * SUF] for u in turned], axis=0).T.astype(jnp.bfloat16)
                q_out[n, :, t * 128 : (t + 1) * 128] = both
                for send in sends:
                    send[n, :HD, t * 128 : (t + 1) * 128] = both


def project(xs, ranks, wq, wk, wv, rope, tails):
    vmem = pl.BlockSpec(memory_space=pltpu.VMEM)
    hbm = pl.BlockSpec(memory_space=pltpu.HBM)
    bf16 = jnp.bfloat16
    outs = [jax.ShapeDtypeStruct((NODES, HD + 16, ROWS), bf16)] * 3
    outs += [jax.ShapeDtypeStruct((NODES, HD, ROWS), bf16), jax.ShapeDtypeStruct((192, 256), bf16)]
    shape = tuple(len(g) for g in xs)
    xs = [a for g in xs for a in g]
    return pl.pallas_call(
        functools.partial(project_kernel, shape),
        out_shape=outs,
        in_specs=[pl.BlockSpec(memory_space=pltpu.SMEM)] + [vmem] * len(xs) + [hbm] * 3 + [vmem] * 3,
        out_specs=[vmem] * 5,
        scratch_shapes=[
            pltpu.VMEM((5, FEATURES, 256), bf16),
            pltpu.VMEM((8, 192, 1024), bf16),
            pltpu.SemaphoreType.DMA((6,)),
        ],
        compiler_params=pltpu.CompilerParams(vmem_limit_bytes=48 * 2**20),
        cost_estimate=pl.CostEstimate(flops=10**6, bytes_accessed=10**6, transcendentals=0),
    )(jnp.stack(ranks).astype(jnp.int32), *xs, wq, wk, wv, *rope, tails)


def attend_kernel(groups, plan, part, idx, steps, keys, *refs):
    refs = list(refs)
    take = lambda n: [refs.pop(0) for _ in range(n)]
    pages = take(len(plan))
    qs = take(len(groups))
    own = groups == (3,)
    suffix = take(1)[0] if own else None
    before = take(3) if part == "far" else None
    outs = [take(2)] if own else [take(3)] if part == "near" else [take(1) for _ in groups]
    pool, q_s, s_a, s_b, acc_s, sems = refs

    copies = []
    for i, (at, ref) in enumerate(zip(plan, pages)):
        copies.append(pltpu.make_async_copy(ref.at[:, 0], pool.at[pl.ds(at, ref.shape[0])], sems.at[i]))
    for copy in copies:
        copy.start()
    for k, q in enumerate(qs):
        q_s[k * NODES : (k + 1) * NODES] = q[:, :HD]
    for copy in copies:
        copy.wait()

    place = lax.broadcasted_iota(jnp.int32, (PAGE, 1), 0)
    over_keys = (((0,), (0,)), ((), ()))
    nodes = len(groups) * NODES

    def scores(n, i, s_ref):
        k = jnp.concatenate([pool[idx[n, i * BLOCK + u], 0] for u in range(BLOCK)], axis=0)
        s_ref[...] = jnp.dot(k, q_s[n], preferred_element_type=jnp.float32)

    def mask(n, i, s_ref):
        left = keys[n] - i * KEYS
        for u in range(BLOCK):

            @pl.when(left < (u + 1) * PAGE)
            def _():
                rows = slice(u * PAGE, (u + 1) * PAGE)
                s_ref[rows] = jnp.where(place < left - u * PAGE, s_ref[rows], LOW)

    def values(n, i, s_ref, peak, total):
        v = jnp.concatenate([pool[idx[n, i * BLOCK + u], 1] for u in range(BLOCK)], axis=0)
        s = s_ref[...]
        old = jnp.where(i == 0, LOW, peak)
        peak = jnp.maximum(old, jnp.max(jnp.max(s.reshape(-1, 8, ROWS), axis=0), axis=0, keepdims=True))
        keep = jnp.exp2((old - peak) * FACTOR)
        w = jnp.exp2(s * FACTOR - peak * FACTOR)
        total = total * keep + jnp.sum(w.reshape(-1, 8, ROWS), axis=0)
        acc_s[...] = acc_s[...] * keep + lax.dot_general(
            v, w.astype(jnp.bfloat16), over_keys, preferred_element_type=jnp.float32
        )
        return peak, total

    def finish(n, peak, total):
        total = jnp.sum(total, axis=0, keepdims=True)
        out = acc_s[...]
        if part == "near":
            outs[0][0][n] = out
            outs[0][1][n] = jnp.broadcast_to(peak, (8, ROWS))
            outs[0][2][n] = jnp.broadcast_to(total, (8, ROWS))
            return
        if part == "far":
            old, old_total = before[1][n, :1], before[2][n, :1]
            both = jnp.maximum(old, peak)
            keep, new = jnp.exp2((old - both) * FACTOR), jnp.exp2((peak - both) * FACTOR)
            out = out * new + before[0][n] * keep
            total = total * new + old_total * keep
            peak = both
        if own:
            r = pl.ds(pl.multiple_of(n * SUF, SUF), SUF)
            s = jnp.dot(suffix[r, :HD], q_s[n], preferred_element_type=jnp.float32)
            key = lax.broadcasted_iota(jnp.int32, (SUF, ROWS), 0)
            query = lax.broadcasted_iota(jnp.int32, (SUF, ROWS), 1) % SUF
            s = jnp.where(key <= query, s, LOW)
            old = peak
            peak = jnp.maximum(jnp.max(s, axis=0, keepdims=True), old)
            keep = jnp.exp2((old - peak) * FACTOR)
            w = jnp.exp2((s - peak) * FACTOR)
            new = lax.dot_general(suffix[r, HD:], w.astype(jnp.bfloat16), over_keys, preferred_element_type=jnp.float32)
            out = out * keep + new
            total = total * keep + jnp.sum(w, axis=0, keepdims=True)
        level = peak * FACTOR + jnp.log2(total)
        out = out * (1.0 / total)
        if own:
            outs[0][0][n] = out
            outs[0][1][n] = jnp.broadcast_to(level, (8, ROWS))
        else:
            high = level.astype(jnp.bfloat16).astype(jnp.float32)
            rest = level - high
            mid = rest.astype(jnp.bfloat16).astype(jnp.float32)
            at = lax.broadcasted_iota(jnp.int32, (16, ROWS), 0)
            tile = jnp.where(at == 0, high, jnp.where(at == 1, mid, jnp.where(at == 2, rest - mid, 0.0)))
            for k in range(len(groups)):

                @pl.when((n >= k * NODES) & (n < (k + 1) * NODES))
                def _():
                    outs[k][0][n - k * NODES, :HD] = out.astype(jnp.bfloat16)
                    outs[k][0][n - k * NODES, HD:] = tile.astype(jnp.bfloat16)

    def after(n, i):
        more = (i + 1 < steps[n]) | (n == nodes - 1)
        return jnp.where(more, n, n + 1), jnp.where(more, i + 1, 0)

    def one(n, i, now, later, peak, total):
        n_next, i_next = after(n, i)
        scores(n_next, jnp.minimum(i_next, MAXP // BLOCK - 1), later)
        peak, total = values(n, jnp.minimum(i, MAXP // BLOCK - 1), now, peak, total)

        @pl.when(i == steps[n] - 1)
        def _():
            finish(n, peak, total)

        @pl.when(i_next >= steps[n_next] - 1)
        def _():
            mask(n_next, i_next, later)

        return n_next, i_next, peak, total

    def two(_, state):
        n, i, peak, total = state
        n, i, peak, total = one(n, i, s_a, s_b, peak, total)
        return one(n, i, s_b, s_a, peak, total)

    acc_s[...] = jnp.zeros_like(acc_s)
    scores(0, 0, s_a)
    mask(0, 0, s_a)
    count = lax.fori_loop(0, nodes, lambda n, c: c + steps[n], 0)
    zero = jnp.int32(0)
    lax.fori_loop(
        0, (count + 1) // 2, two, (zero, zero, jnp.full((1, ROWS), LOW, jnp.float32), jnp.zeros((8, ROWS), jnp.float32))
    )


def attend(groups, lists, pages, qs, suffix, part=None, before=()):
    own = groups == (3,)
    f32 = jnp.float32
    if own:
        outs = [jax.ShapeDtypeStruct((NODES, HD, ROWS), f32), jax.ShapeDtypeStruct((NODES, 8, ROWS), f32)]
    elif part == "near":
        outs = [jax.ShapeDtypeStruct((len(groups) * NODES, d, ROWS), f32) for d in (HD, 8, 8)]
    else:
        outs = [jax.ShapeDtypeStruct((NODES, HD + 16, ROWS), jnp.bfloat16) for _ in groups]
    n = len(groups) * NODES
    extra = ([suffix] if own else []) + list(before)
    vmem = pl.BlockSpec(memory_space=pltpu.VMEM)
    smem = pl.BlockSpec(memory_space=pltpu.SMEM)
    hbm = pl.BlockSpec(memory_space=pl.ANY)
    return pl.pallas_call(
        functools.partial(attend_kernel, groups, tuple(at for at, _ in pages), part),
        out_shape=outs,
        in_specs=[smem] * 3 + [hbm] * len(pages) + [vmem] * (len(qs) + len(extra)),
        out_specs=[vmem] * len(outs),
        scratch_shapes=[
            pltpu.VMEM((sum(a.shape[0] for _, a in pages), 2, PAGE, HD), jnp.bfloat16),
            pltpu.VMEM((n, HD, ROWS), jnp.bfloat16),
            pltpu.VMEM((KEYS, ROWS), f32),
            pltpu.VMEM((KEYS, ROWS), f32),
            pltpu.VMEM((HD, ROWS), f32),
            pltpu.SemaphoreType.DMA((len(pages),)),
        ],
        compiler_params=pltpu.CompilerParams(vmem_limit_bytes=(52 if own else 36) * 2**20),
        cost_estimate=pl.CostEstimate(flops=10**9, bytes_accessed=10**6, transcendentals=0),
    )(*lists, *[a for _, a in pages], *qs, *extra)


def merge_kernel(o_ref, l_ref, a_ref, b_ref, c_ref, out_ref):
    others = [a_ref, b_ref, c_ref]
    for n in range(NODES):
        levels = [l_ref[n, :1]]
        for r in others:
            t = r[n, HD:].astype(jnp.float32)
            levels.append(t[0:1] + t[1:2] + t[2:3])
        top = functools.reduce(jnp.maximum, levels)
        weights = [jnp.exp2(v - top) for v in levels]
        share = 1.0 / functools.reduce(jnp.add, weights)
        out = o_ref[n] * (weights[0] * share)
        for w, r in zip(weights[1:], others):
            out = out + r[n, :HD].astype(jnp.float32) * (w * share)
        rows = slice(n * SUF, (n + 1) * SUF)
        for t in range(HEADS // 2):
            both = out[:, t * 128 : (t + 1) * 128].T.astype(jnp.bfloat16)
            out_ref[rows, 2 * t * HD : (2 * t + 1) * HD] = both[:SUF]
            out_ref[rows, (2 * t + 1) * HD : (2 * t + 2) * HD] = both[SUF:]


def make_lists(mask, where, lens):
    place = jnp.arange(MAXP, dtype=jnp.int32)
    upto = jnp.sum(jnp.where(place[None, None, :] <= place[None, :, None], mask[:, None, :], False).astype(jnp.int32), axis=-1)
    hit = mask[:, None, :] & (upto[:, None, :] - 1 == place[None, :, None])
    idx = jnp.sum(jnp.where(hit, where[:, None, :], 0), axis=-1)
    count = jnp.sum(mask.astype(jnp.int32), axis=-1)
    keys = jnp.sum(jnp.where(mask, jnp.minimum(PAGE, lens[:, None] - place[None, :] * PAGE), 0), axis=-1)
    return idx, jnp.maximum((count + BLOCK - 1) // BLOCK, 1), keys


def body(tokens, w_query, w_key, w_value, kv_pool, page_owner, page_slot, prefix_len):
    pool_at, tp_at = lax.axis_index("pool"), lax.axis_index("tp")
    x, y, core = pool_at // 4, pool_at % 4, tp_at % 2
    along_page = jnp.where(core == 0, y, x)
    along_query = jnp.where(core == 0, x, y)
    move = lambda a, perm: lax.ppermute(a, AX, perm)

    tok_a, tok_b = move(tokens, z_shift(1)), move(tokens, z_shift(-1))
    tok_o = move(tokens, core_swap())
    page_a, page_b = move(kv_pool, page_shift(1)), move(kv_pool, page_shift(-1))

    positions = (prefix_len[:, None] + jnp.arange(SUF, dtype=jnp.int32)[None, :]).astype(jnp.float32).reshape(192, 1)
    inverse = rope_base ** (-(jnp.arange(HD // 2, dtype=jnp.float32) * 2.0 / HD))
    angles = positions * inverse
    cosine, sine = jnp.cos(angles), jnp.sin(angles)
    rope = (jnp.concatenate([cosine, cosine], axis=1), jnp.concatenate([-sine, sine], axis=1))

    owner = page_owner[..., 0]
    owner_page = jnp.where(core == 0, owner % 4, owner // 4)
    owner_query = jnp.where(core == 0, owner // 4, owner % 4)
    apart = (owner_page - along_page) % 4
    start = jnp.where(apart == 0, 0, jnp.where(apart == 3, 64, jnp.where(apart == 1, 128, 192)))
    valid = jnp.arange(MAXP, dtype=jnp.int32)[None, :] * PAGE < prefix_len[:, None]
    places = [valid & (owner_query == (along_query + d) % 4) for d in (1, -1, 2, 0)]
    masks = [m & (apart != 2) for m in places[:3]] + [m & (apart == 2) for m in places[:3]] + places[3:]
    where = [start + page_slot] * 3 + [page_slot] * 3 + [start + page_slot]
    idx, steps, keys = make_lists(jnp.concatenate(masks, axis=0), jnp.concatenate(where, axis=0), jnp.tile(prefix_len, 7))
    numbers = jnp.stack([steps, keys // 64, keys % 64], axis=-1)
    numbers = jnp.pad(numbers, ((0, 0), (0, MAXP - 3)))
    tails = jnp.stack([idx[:9], numbers[:9], idx[9:18], numbers[9:18]], axis=1).astype(jnp.bfloat16)
    tails = jnp.pad(tails, ((0, 0), (0, 12), (0, ROWS - MAXP)))
    tails = tails.reshape(3, NODES, 16, ROWS)

    tok_a, tok_b, tails, rope = lax.optimization_barrier((tok_a, tok_b, tails, rope))
    tok_ao, tok_bo = move(tok_a, core_swap()), move(tok_b, core_swap())
    tok_c, tok_d = move(tok_a[:96], z_shift(1)), move(tok_b[96:], z_shift(-1))
    tok_co, tok_do = move(tok_c, core_swap()), move(tok_d, core_swap())
    z = tp_at // 2
    rank = lambda dz, same: ((z + dz) % 4) * 2 + (core if same else 1 - core)
    blocks = [[tokens], [tok_o], [tok_a], [tok_b], [tok_ao], [tok_bo], [tok_c, tok_d], [tok_co, tok_do]]
    ranks = [rank(dz, same) for dz, same in ((0, 1), (0, 0), (-1, 1), (1, 1), (-1, 0), (1, 0), (2, 1), (2, 0))]
    *sends, queries, suffix = project(blocks, ranks, w_query, w_key, w_value, rope, tails)
    suffix_kv = suffix.reshape(192, 2, 1, HD)

    qs = [move(sends[1], query_shift(-1)), move(sends[0], query_shift(1)), move(sends[2], query_shift(2))]
    page_al, page_bh, *qs = lax.optimization_barrier((page_a[:32], page_b[32:], *qs))
    page_c, page_d = move(page_al, page_shift(1)), move(page_bh, page_shift(-1))
    got = jnp.concatenate([q[:, HD : HD + 4, :MAXP] for q in qs], axis=0).astype(jnp.int32)
    near, far = ((got[:, i], got[:, i + 1, 0], got[:, i + 1, 1] * 64 + got[:, i + 1, 2]) for i in (0, 2))
    pages = ((0, kv_pool), (64, page_a), (128, page_b), (192, page_c), (224, page_d))
    others = (0, 1, 2)
    before = attend(others, near, pages[:3], qs, None, "near")
    sent = attend(others, far, ((0, page_c), (32, page_d)), qs, None, "far", before)
    back = [move(r, query_shift(s)) for r, s in zip(sent, (1, -1, 2))]
    mine = attend((3,), (idx[18:], steps[18:], keys[18:]), pages, [queries], suffix)
    attended = pl.pallas_call(
        merge_kernel,
        out_shape=jax.ShapeDtypeStruct((192, 1024), jnp.bfloat16),
        compiler_params=pltpu.CompilerParams(vmem_limit_bytes=16 * 2**20),
    )(*mine, *back)
    return attended, suffix_kv


def solution(mesh):
    in_specs = (
        P("pool", "tp"),
        P(None, "tp"),
        P(None, "tp"),
        P(None, "tp"),
        P("pool", "tp", None, None, None),
        P("pool", None, None),
        P("pool", None),
        P("pool"),
    )
    out_specs = (P("pool", "tp"), P("pool", None, "tp", None))
    return jax.shard_map(body, mesh=mesh, in_specs=in_specs, out_specs=out_specs, check_vma=False)
```
